32 devices in a mesh: rep: 2 (over y), mem: 4 (over x, core), grid: 4 (over z).
Axes of the slice: x: 2, y: 2, z: 4, core: 2. Of those that a mesh axis runs over, the one named last changes fastest.
Arguments:
- grid_hidden_state: bfloat16 [8, 1536, 1024], P(('rep', 'mem'), 'grid'), parts along dimension 0, may hold values from -6 to 6
- mesh_node_keys: bfloat16 [8, 512, 1024], P(('rep', 'mem'), 'grid'), parts along dimension 0, may hold values from -6 to 6
- mesh_node_values: bfloat16 [8, 512, 1024], P(('rep', 'mem'), 'grid'), parts along dimension 0, may hold values from -6 to 6
- query_weight: bfloat16 [1024, 1024], replicated, may hold values from -0.1875 to 0.1875
- head_weight: bfloat16 [1024, 100], replicated, may hold values from -0.1875 to 0.1875
- rms_norm_gain: float32 [1024], replicated, may hold values from 0.5 to 1.5
- edge_bias: float32 [3, 16, 1536], P(None, None, 'grid'), may hold values from -6 to 450
- send_rows: int32 [4, 4, 4], P('grid'), may hold values from 0 to 127, as said below
- edge_src: int32 [3, 1536], P(None, 'grid'), may hold values from 0 to 15, as said below
- targets: float32 [200, 1536], P('rep', 'grid'), parts along dimension 0, may hold values from -6 to 6
- point_area_weight: float32 [1536], P('grid'), may hold values from 1 to 10
- variable_loss_weight: float32 [100], replicated, may hold values from 0.5 to 5
Outputs:
- grid_latent_gradient: bfloat16 [8, 1536, 1024], P(('rep', 'mem'), 'grid'), parts along dimension 0
- mesh_key_gradient: bfloat16 [8, 512, 1024], P(('rep', 'mem'), 'grid'), parts along dimension 0
- mesh_value_gradient: bfloat16 [8, 512, 1024], P(('rep', 'mem'), 'grid'), parts along dimension 0
- head_weight_gradient: float32 [8, 1024, 100], P(('rep', 'mem'), 'grid'), parts along dimension 0
The draws below stay inside these ranges and needn't reach their ends.
There are 2 independent parts, one for each index of `rep`. The reference program is written for one: setup_inputs(seed, part) draws one part's arguments, and reference() takes and returns one part's arrays. A program takes and returns all parts, laid end to end along the dimension named above; an argument that names none is the same for every part. Nothing has to cross between parts.
Inputs may be any that keep to these rules, and one draw needn't show every extreme that they name: send_rows[s, d] lists, in its first slots, distinct mesh rows of shard s (indices inside its block of 128) that receiver shard d reads; the other slots hold 0 and no edge reads them; for some receiver shard every slot of every sender is in use. edge_src[k, g] = s * 4 + j names slot j of sender shard s's list for the receiver shard of g; every slot in use is read by some edge of that receiver, no unused slot is read.
All inputs are finite; a program needn't handle non-finite values.
Results may differ from the reference program's by a relative error of at most 0.011.
Values may be sent and summed in bfloat16 or wider, within the bound.
A program may use at most 64 MiB of HBM per device.

```python
import math
import jax
import jax.numpy as jnp
from jax import lax

C = 1024
H = 16
V = 100
K = 3
CAP = 4
G_DEV = 384
M_DEV = 128
MEMBER_COUNT = 4
NG = 1536
NM = 512
N_GRID = 4


def graph_tables(key):
    key_count, key_busy, key_offset, key_order, key_spare = jax.random.split(jax.random.fold_in(key, 101), 5)
    counts = jax.random.randint(key_count, (N_GRID, N_GRID), 1, CAP + 1)
    busiest = jax.random.randint(key_busy, (), 0, N_GRID)
    column = jnp.arange(N_GRID, dtype=jnp.int32)
    counts = jnp.where(column[None, :] == busiest, CAP, counts)
    offset = jax.random.randint(key_offset, (N_GRID, N_GRID), 0, M_DEV)
    corner = (column[:, None] == 0) & (column[None, :] == busiest)
    offset = jnp.where(corner, M_DEV - 1, offset)
    slot_index = jnp.arange(CAP, dtype=jnp.int32)
    row_index = (offset[:, :, None] + slot_index[None, None, :] * (M_DEV // CAP)) % M_DEV
    in_use = slot_index[None, None, :] < counts[:, :, None]
    send_table = jnp.where(in_use, row_index, 0).astype(jnp.int32)
    use_by_receiver = jnp.transpose(in_use, (1, 0, 2)).reshape(N_GRID, N_GRID * CAP)
    flat_slots = jnp.arange(N_GRID * CAP, dtype=jnp.int32)
    ranking = jnp.where(use_by_receiver, flat_slots[None, :], flat_slots[None, :] + N_GRID * CAP)
    ordering = jnp.argsort(ranking, axis=1).astype(jnp.int32)
    live_slots = jnp.sum(use_by_receiver.astype(jnp.int32), axis=1)
    edge_total = K * G_DEV
    order_keys = jax.random.split(key_order, N_GRID)
    position = jax.vmap(lambda single: jax.random.permutation(single, edge_total))(order_keys).astype(jnp.int32)
    spare_pick = jax.random.randint(key_spare, (N_GRID, edge_total), 0, 1048576) % live_slots[:, None]
    slot_rank = jnp.where(position < live_slots[:, None], position, spare_pick)
    chosen = jnp.take_along_axis(ordering, slot_rank, axis=1).astype(jnp.int32)
    edge_table = jnp.transpose(chosen.reshape(N_GRID, K, G_DEV), (1, 0, 2)).reshape(K, N_GRID * G_DEV)
    return (send_table, edge_table)


def draw_send_rows(key, part):
    return graph_tables(key)[0]


def draw_edge_src(key, part):
    return graph_tables(key)[1]


def draw_edge_bias(key, part):
    key = jax.random.fold_in(key, 7)
    first = jax.random.fold_in(key, 0)
    bias_shape = (K, H, N_GRID * G_DEV)
    return jnp.clip(1.5 * jax.random.normal(first, bias_shape, jnp.float32), -6.0, 6.0)


def block_scale(key, dims, shards, smallest, high):
    def one(axis_at, blocks):
        heights = jax.random.uniform(jax.random.fold_in(jax.random.fold_in(key, 6), axis_at), (blocks,), jnp.float32, smallest / len(shards), high / len(shards))
        return jnp.repeat(jnp.exp(heights), dims[axis_at] // blocks).reshape((-1,) + (1,) * (len(dims) - axis_at - 1))

    level = one(*shards[0])
    for cut in shards[1:]:
        level = level * one(*cut)
    return level


def centred(key, shape, scale, most, shards=(), kind=jnp.bfloat16):
    array = jax.random.normal(key, shape, jnp.float32) * scale
    if len(shards) > 0:
        array = block_scale(key, shape, shards, -0.22, 0.18) * array
    return jnp.clip(array, min=-most, max=most).astype(kind)


def setup_inputs(seed: int = 0, part: int = 0) -> dict:
    key_list = jax.random.split(jax.random.key(seed), 13)
    own_keys = jax.random.split(jax.random.fold_in(key_list[12], part), 13)
    grid_hidden_state = centred(own_keys[0], (MEMBER_COUNT, NG, C), 1.0, 6.0, ((0, 4), (1, 4)))
    mesh_node_keys = centred(own_keys[1], (MEMBER_COUNT, NM, C), 1.0, 6.0, ((0, 4), (1, 4)))
    mesh_node_values = centred(own_keys[2], (MEMBER_COUNT, NM, C), 1.0, 6.0, ((0, 4), (1, 4)))
    query_weight = centred(key_list[3], (C, C), C ** -0.5, 0.1875)
    head_weight = centred(key_list[4], (C, V), C ** -0.5, 0.1875)
    rms_norm_gain = jnp.clip(1.0 + 0.1 * jax.random.normal(key_list[5], (C,), jnp.float32), 0.5, 1.5)
    edge_bias = draw_edge_bias(jax.random.fold_in(key_list[12], 71), part)
    send_rows = draw_send_rows(jax.random.fold_in(key_list[12], 71), part)
    edge_src = draw_edge_src(jax.random.fold_in(key_list[12], 71), part)
    targets = centred(own_keys[9], (V, NG), 1.0, 6.0, ((1, 4),), jnp.float32)
    point_area_weight = jnp.clip(jnp.exp(math.log(10.0) - 2.3025851 * jax.random.uniform(key_list[10], (NG,), jnp.float32) ** block_scale(key_list[10], (NG,), ((0, 4),), -0.2, 0.2)), 1.0, 10.0)
    variable_loss_weight = jnp.clip(jnp.exp(jax.random.uniform(key_list[11], (V,), jnp.float32, math.log(0.5), math.log(5.0))), 0.5, 5.0)
    return dict(grid_hidden_state=grid_hidden_state, mesh_node_keys=mesh_node_keys, mesh_node_values=mesh_node_values, query_weight=query_weight, head_weight=head_weight, rms_norm_gain=rms_norm_gain, edge_bias=edge_bias, send_rows=send_rows, edge_src=edge_src, targets=targets, point_area_weight=point_area_weight, variable_loss_weight=variable_loss_weight)


TAU = 0.1
EPS = 1e-06

def soft_sign_value(value):
    return value / jnp.sqrt(value * value + TAU * TAU)

def forward_for_member(hidden_state, member_keys, member_values, query_weight, head_weight, rms_norm_gain, edge_bias_table, sender_row):
    query = jnp.dot(hidden_state, query_weight, preferred_element_type=jnp.float32).astype(jnp.bfloat16)
    points = hidden_state.shape[0]
    head_size = hidden_state.shape[1] // H
    query_float_rows = query.astype(jnp.float32).reshape(points, H, head_size)
    keys_float = member_keys[sender_row].astype(jnp.float32).reshape(K, points, H, head_size)
    values_float = member_values[sender_row].astype(jnp.float32).reshape(K, points, H, head_size)
    scores = jnp.einsum('ghd,kghd->kgh', query_float_rows, keys_float) / math.sqrt(head_size) + edge_bias_table
    attention_weights = jax.nn.softmax(scores, axis=0)
    attended = jnp.einsum('kgh,kghd->ghd', attention_weights, values_float).reshape(points, -1)
    merged_output = hidden_state.astype(jnp.float32) + attended
    inverse_rms = 1.0 / jnp.sqrt(lax.optimization_barrier(jnp.mean(merged_output * merged_output, axis=1, keepdims=True)) + EPS)
    normalized_latent = (merged_output * inverse_rms * rms_norm_gain).astype(jnp.bfloat16)
    member_prediction = lax.dot_general(head_weight, normalized_latent, (((0,), (1,)), ((), ())), preferred_element_type=jnp.float32)
    return (query_float_rows, keys_float, values_float, attention_weights, merged_output, inverse_rms, normalized_latent, member_prediction)

def reference(grid_hidden_state, mesh_node_keys, mesh_node_values, query_weight, head_weight, rms_norm_gain, edge_bias, send_rows, edge_src, targets, point_area_weight, variable_loss_weight):
    receiver = (jnp.arange(NG, dtype=jnp.int32) // G_DEV)[None, :]
    sender = edge_src // CAP
    slot_of = edge_src % CAP
    sender_row = (sender * M_DEV + send_rows[sender, receiver, slot_of]).astype(jnp.int32)
    slot_id = (receiver * (N_GRID * CAP) + edge_src).reshape(-1).astype(jnp.int32)
    owner = (jnp.arange(N_GRID, dtype=jnp.int32)[None, :, None] * M_DEV + jnp.transpose(send_rows, (1, 0, 2))).reshape(-1).astype(jnp.int32)
    edge_bias_table = jnp.transpose(edge_bias, (0, 2, 1))

    def prediction_alone(member_index):
        return forward_for_member(member_index[0], member_index[1], member_index[2], query_weight, head_weight, rms_norm_gain, edge_bias_table, sender_row)[-1]
    ensemble_predictions = lax.map(prediction_alone, (grid_hidden_state, mesh_node_keys, mesh_node_values))

    def spread_between(member_prediction):
        pairwise_terms = lax.optimization_barrier(jnp.sum(soft_sign_value(member_prediction[None] - ensemble_predictions), axis=0))
        return soft_sign_value(member_prediction - targets) / MEMBER_COUNT - pairwise_terms / (MEMBER_COUNT * (MEMBER_COUNT - 1))
    ensemble_spread = lax.map(spread_between, ensemble_predictions)
    prediction_gradient = (point_area_weight[None, None, :] * variable_loss_weight[None, :, None] * ensemble_spread).astype(jnp.bfloat16)

    def backward_for_member(member_index):
        hidden_state, member_keys, member_values, grad_pred = member_index
        query_float_rows, keys_float, values_float, attention_weights, merged_output, inverse_rms, normalized_latent, member_prediction = forward_for_member(hidden_state, member_keys, member_values, query_weight, head_weight, rms_norm_gain, edge_bias_table, sender_row)
        points = hidden_state.shape[0]
        head_size = hidden_state.shape[1] // H
        head_weight_gradient = lax.dot_general(normalized_latent, grad_pred, (((0,), (1,)), ((), ())), preferred_element_type=jnp.float32) * (1.0 / math.sqrt(NG))
        grad_normed = lax.dot_general(grad_pred, head_weight, (((0,), (1,)), ((), ())), preferred_element_type=jnp.float32)
        gained = grad_normed * rms_norm_gain
        grad_combined = inverse_rms * gained - merged_output * inverse_rms ** 3 * lax.optimization_barrier(jnp.mean(gained * merged_output, axis=1, keepdims=True))
        grad_heads = grad_combined.reshape(points, H, head_size)
        grad_weights = jnp.einsum('ghd,kghd->kgh', grad_heads, values_float)
        grad_scores = attention_weights * (grad_weights - lax.optimization_barrier(jnp.sum(attention_weights * grad_weights, axis=0, keepdims=True)))
        grad_query = (jnp.einsum('kgh,kghd->ghd', grad_scores, keys_float) / math.sqrt(head_size)).reshape(points, -1).astype(jnp.bfloat16)
        grid_latent_gradient = (grad_combined + lax.dot_general(grad_query, query_weight, (((1,), (1,)), ((), ())), preferred_element_type=jnp.float32)).astype(jnp.bfloat16)
        edge_grad_keys = (jnp.einsum('kgh,ghd->kghd', grad_scores, query_float_rows) / math.sqrt(head_size)).astype(jnp.bfloat16).reshape(K * points, -1)
        edge_grad_values = jnp.einsum('kgh,ghd->kghd', attention_weights, grad_heads).astype(jnp.bfloat16).reshape(K * points, -1)
        slot_keys = jax.ops.segment_sum(edge_grad_keys.astype(jnp.float32), slot_id, N_GRID * N_GRID * CAP).astype(jnp.bfloat16)
        slot_values = jax.ops.segment_sum(edge_grad_values.astype(jnp.float32), slot_id, N_GRID * N_GRID * CAP).astype(jnp.bfloat16)
        mesh_key_gradient = jax.ops.segment_sum(slot_keys.astype(jnp.float32), owner, NM).astype(jnp.bfloat16)
        mesh_value_gradient = jax.ops.segment_sum(slot_values.astype(jnp.float32), owner, NM).astype(jnp.bfloat16)
        return (grid_latent_gradient, mesh_key_gradient, mesh_value_gradient, head_weight_gradient)
    grid_latent_gradient, mesh_key_gradient, mesh_value_gradient, head_weight_gradient = lax.map(backward_for_member, (grid_hidden_state, mesh_node_keys, mesh_node_values, prediction_gradient))
    return (grid_latent_gradient, mesh_key_gradient, mesh_value_gradient, head_weight_gradient)
```

```python
import functools
import math

import jax
import jax.numpy as jnp
from jax import lax
from jax.experimental import pallas as pl
from jax.experimental.pallas import tpu as pltpu
from jax.sharding import PartitionSpec as P

H = 16
K = 3
TAU = 0.1
EPS = 1e-06
LANES = 128
F32 = jnp.float32
BF16 = jnp.bfloat16
MESH = pl.DeviceIdType.MESH


def phi(value):
    return value * lax.rsqrt(value * value + TAU * TAU)


def mm(a, b, ca=1, cb=0):
    return lax.dot_general(a, b, (((ca,), (cb,)), ((), ())), preferred_element_type=F32)


def iota(shape, axis):
    return lax.broadcasted_iota(jnp.int32, shape, axis)


def ring_copies(src, dst, send_sem, recv_sem, axis, me, count):
    copies = []
    for step in range(1, count):
        peer = lax.rem(me + step, count)
        copies.append(
            pltpu.make_async_remote_copy(
                src_ref=src(peer),
                dst_ref=dst(me),
                send_sem=send_sem.at[step],
                recv_sem=recv_sem.at[step],
                device_id={axis: peer},
                device_id_type=MESH,
            )
        )
    return copies


def kernel(
    n,
    m,
    hidden,
    keys,
    values,
    wq,
    hw,
    gain_ref,
    bias,
    send_rows,
    edge_src,
    targets,
    area,
    var_weight,
    out_latent,
    out_keys,
    out_values,
    out_head,
    kv_send,
    kv_recv,
    back_send,
    back_recv,
    f_send,
    f_recv,
    hw_send,
    hw_recv,
    hw_own,
    q_ref,
    hwt,
    rows_ref,
    kb,
    vb,
    kbw,
    score_ref,
    w_ref,
    p_hi,
    p_lo,
    gs_ref,
    combined_ref,
    normed_ref,
    f_ref,
    pg_ref,
    gc_ref,
    gcb_ref,
    kv_sems,
    back_sems,
    f_sems,
    hw_sems,
):
    me = lax.axis_index("grid")
    member = lax.axis_index("mem")
    points, features = hidden.shape[1], hidden.shape[2]
    head = features // H
    per_tile = LANES // head
    cap = send_rows.shape[2]
    pair = 2 * cap
    slots = n * cap
    rows = n * pair
    half = features // 2
    nvar = hw.shape[1]
    vpad = hwt.shape[0]
    mesh_rows = keys.shape[1]
    chunks = points // LANES
    hcols = features // n

    table = send_rows[0].astype(F32).astype(BF16)
    spread_rows = jnp.where(iota((rows, n), 0) // pair == iota((rows, n), 1), 1.0, 0.0).astype(BF16)
    picked = mm(spread_rows, table)
    column = iota((rows, cap), 0) % cap == iota((rows, cap), 1)
    flat = jnp.sum(jnp.where(column, picked, 0.0), axis=1, keepdims=True)
    hit = iota((rows, mesh_rows), 1).astype(F32) == flat
    is_key = iota((rows, mesh_rows), 0) % pair < cap
    pick_key = jnp.where(hit & is_key, 1.0, 0.0).astype(BF16)
    pick_value = jnp.where(hit & ~is_key, 1.0, 0.0).astype(BF16)
    gathered = mm(pick_key, keys[0]) + mm(pick_value, values[0])

    def pack(block):
        return jnp.concatenate([block[:, :half], block[:, half:]], axis=0).astype(BF16)

    for d in range(n):
        kv_send[d] = pack(gathered[d * pair : (d + 1) * pair])

    barrier = pltpu.get_barrier_semaphore()
    for step in range(1, n):
        pl.semaphore_signal(
            barrier, inc=1, device_id={"grid": lax.rem(me + step, n)}, device_id_type=MESH
        )
    for step in range(1, m):
        pl.semaphore_signal(
            barrier, inc=1, device_id={"mem": lax.rem(member + step, m)}, device_id_type=MESH
        )
    pl.semaphore_wait(barrier, n + m - 2)

    kv_copies = ring_copies(
        lambda peer: kv_send.at[peer],
        lambda mine: kv_recv.at[mine],
        kv_sems.at[0],
        kv_sems.at[1],
        "grid",
        me,
        n,
    )
    for copy in kv_copies:
        copy.start()
    kv_recv[me] = kv_send[me]

    q_ref[...] = mm(hidden[0], wq[...]).astype(BF16)
    hwt[...] = jnp.zeros_like(hwt)
    hwt[:nvar, :] = jnp.transpose(hw[...].astype(F32)).astype(BF16)
    kb[...] = jnp.zeros_like(kb)
    vb[...] = jnp.zeros_like(vb)
    gain = gain_ref[...]
    vw = jnp.sum(
        jnp.where(iota((vpad, nvar), 0) == iota((vpad, nvar), 1), var_weight[...], 0.0),
        axis=1,
        keepdims=True,
    )

    for copy in kv_copies:
        copy.wait_recv()
    for s in range(n):
        block = kv_recv[s].astype(F32)
        rows_ref[s * pair : (s + 1) * pair, :half] = block[:pair]
        rows_ref[s * pair : (s + 1) * pair, half:] = block[pair:]
    received = rows_ref[...].astype(BF16)
    slot_at = iota((slots, rows), 0)
    slot_row = slot_at // cap * pair + slot_at % cap
    at_key = jnp.where(iota((slots, rows), 1) == slot_row, 1.0, 0.0).astype(BF16)
    at_value = jnp.where(iota((slots, rows), 1) == slot_row + cap, 1.0, 0.0).astype(BF16)
    slot_k = mm(at_key, received)
    slot_v = mm(at_value, received)
    which = iota((slots, LANES), 1) // head
    for h in range(H):
        tile = slice(h // per_tile * LANES, (h // per_tile + 1) * LANES)
        mine = which == h % per_tile
        kb[h * slots : (h + 1) * slots, tile] = jnp.where(mine, slot_k[:, tile], 0.0).astype(BF16)
        vb[h * slots : (h + 1) * slots, tile] = jnp.where(mine, slot_v[:, tile], 0.0).astype(BF16)

    def onehots(at):
        slot = iota((slots, LANES), 0)
        return [slot == edge_src[k : k + 1, at] for k in range(K)]

    def select(table, hots, at):
        for h in range(H):
            part = table[h * slots : (h + 1) * slots]
            for k in range(K):
                score_ref[k, h : h + 1, at] = jnp.sum(
                    jnp.where(hots[k], part, 0.0), axis=0, keepdims=True
                )

    scale = 1.0 / math.sqrt(head)
    inverse = []
    f_copies = []
    for c in range(chunks):
        at = slice(c * LANES, (c + 1) * LANES)
        hots = onehots(at)
        select(mm(kb[...], q_ref[at, :], 1, 1), hots, at)
        scores = [score_ref[k, :, at] * scale + bias[k, :, at] for k in range(K)]
        top = functools.reduce(jnp.maximum, scores)
        exps = [jnp.exp(s - top) for s in scores]
        total = functools.reduce(jnp.add, exps)
        for k in range(K):
            w_ref[k, :, at] = exps[k] / total
        for h in range(H):
            block = functools.reduce(
                jnp.add,
                [jnp.where(hots[k], w_ref[k, h : h + 1, at], 0.0) for k in range(K)],
            )
            high = block.astype(BF16)
            p_hi[h * slots : (h + 1) * slots, at] = high
            p_lo[h * slots : (h + 1) * slots, at] = (block - high.astype(F32)).astype(BF16)
        attended = mm(p_hi[:, at], vb[...], 0, 0) + mm(p_lo[:, at], vb[...], 0, 0)
        combined = hidden[0, at, :].astype(F32) + attended
        inv = lax.rsqrt(jnp.mean(combined * combined, axis=1, keepdims=True) + EPS)
        inverse.append(inv)
        combined_ref[at, :] = combined
        normed_ref[at, :] = (combined * inv * gain).astype(BF16)
        forecast = mm(hwt[...], normed_ref[at, :], 1, 1)
        f_ref[:, at] = forecast
        f_send[c] = forecast.astype(BF16)
        copies = ring_copies(
            lambda peer, c=c: f_send.at[c],
            lambda mine, c=c: f_recv.at[c, mine],
            f_sems.at[0, c],
            f_sems.at[1, c],
            "mem",
            member,
            m,
        )
        for copy in copies:
            copy.start()
        f_copies.append(copies)

    kbw[...] = mm(kb[...], wq[...], 1, 1).astype(BF16)

    for c in range(chunks):
        at = slice(c * LANES, (c + 1) * LANES)
        for copy in f_copies[c]:
            copy.wait_recv()
        forecast = f_ref[:, at]
        pairwise = jnp.zeros_like(forecast)
        for step in range(1, m):
            other = f_recv[c, lax.rem(member + step, m)].astype(F32)
            pairwise = pairwise + phi(forecast - other)
        pairwise = pairwise[:nvar]
        spread = phi(forecast[:nvar] - targets[:, at]) / m - pairwise / (m * (m - 1))
        pg_ref[:nvar, at] = (area[:, at] * vw[:nvar] * spread).astype(BF16)
        pg_ref[nvar:, at] = jnp.zeros((vpad - nvar, LANES), BF16)

    head_part = mm(pg_ref[...], normed_ref[...]) * (1.0 / math.sqrt(points * n))
    for d in range(n):
        part = head_part[:, d * hcols : (d + 1) * hcols]
        hw_own[d] = part
        hw_send[d] = part.astype(BF16)
    hw_copies = ring_copies(
        lambda peer: hw_send.at[peer],
        lambda mine: hw_recv.at[mine],
        hw_sems.at[0],
        hw_sems.at[1],
        "grid",
        me,
        n,
    )
    for copy in hw_copies:
        copy.start()

    for c in range(chunks):
        at = slice(c * LANES, (c + 1) * LANES)
        hots = onehots(at)
        inv = inverse[c]
        combined = combined_ref[at, :]
        gained = mm(pg_ref[:, at], hwt[...], 0, 0) * gain
        along = jnp.mean(gained * combined, axis=1, keepdims=True)
        grad = inv * gained - combined * (inv * inv * inv * along)
        gc_ref[at, :] = grad
        gcb_ref[at, :] = grad.astype(BF16)
        select(mm(vb[...], gcb_ref[at, :], 1, 1), hots, at)
        grads = [score_ref[k, :, at] for k in range(K)]
        ws = [w_ref[k, :, at] for k in range(K)]
        centre = functools.reduce(jnp.add, [w * g for w, g in zip(ws, grads)])
        for k in range(K):
            score_ref[k, :, at] = ws[k] * (grads[k] - centre) * scale
        for h in range(H):
            block = functools.reduce(
                jnp.add,
                [jnp.where(hots[k], score_ref[k, h : h + 1, at], 0.0) for k in range(K)],
            )
            gs_ref[h * slots : (h + 1) * slots, at] = block.astype(BF16)

    slot_k_grad = mm(gs_ref[...], q_ref[...])
    slot_v_grad = mm(p_hi[...], gcb_ref[...])

    def own_heads(table):
        tiles = []
        for t in range(features // LANES):
            tile = slice(t * LANES, (t + 1) * LANES)
            value = None
            for i in range(per_tile):
                h = t * per_tile + i
                part = table[h * slots : (h + 1) * slots, tile]
                value = part if value is None else jnp.where(which == i, part, value)
            tiles.append(value)
        return jnp.concatenate(tiles, axis=1).astype(BF16)

    back = mm(at_key, own_heads(slot_k_grad), 0, 0) + mm(at_value, own_heads(slot_v_grad), 0, 0)
    for d in range(n):
        back_send[d] = pack(back[d * pair : (d + 1) * pair])
    back_copies = ring_copies(
        lambda peer: back_send.at[peer],
        lambda mine: back_recv.at[mine],
        back_sems.at[0],
        back_sems.at[1],
        "grid",
        me,
        n,
    )
    for copy in back_copies:
        copy.start()
    back_recv[me] = back_send[me]

    for c in range(chunks):
        at = slice(c * LANES, (c + 1) * LANES)
        out_latent[0, at, :] = (gc_ref[at, :] + mm(gs_ref[:, at], kbw[...], 0, 0)).astype(BF16)

    for copy in hw_copies:
        copy.wait_recv()
    total = hw_own[me]
    for step in range(1, n):
        total = total + hw_recv[lax.rem(me + step, n)].astype(F32)
    out_head[0] = jnp.transpose(total)[:, :nvar]

    for copy in back_copies:
        copy.wait_recv()
    for s in range(n):
        block = back_recv[s].astype(F32)
        rows_ref[s * pair : (s + 1) * pair, :half] = block[:pair]
        rows_ref[s * pair : (s + 1) * pair, half:] = block[pair:]
    returned = rows_ref[...].astype(BF16)
    out_keys[0] = mm(pick_key, returned, 0, 0).astype(BF16)
    out_values[0] = mm(pick_value, returned, 0, 0).astype(BF16)

    for copies in [kv_copies, hw_copies, back_copies] + f_copies:
        for copy in copies:
            copy.wait_send()


def shards(
    grid_hidden_state,
    mesh_node_keys,
    mesh_node_values,
    query_weight,
    head_weight,
    rms_norm_gain,
    edge_bias,
    send_rows,
    edge_src,
    targets,
    point_area_weight,
    variable_loss_weight,
):
    n = lax.axis_size("grid")
    m = lax.axis_size("mem")
    points, features = grid_hidden_state.shape[1:]
    nvar = head_weight.shape[1]
    vpad = -(-nvar // 16) * 16
    cap = send_rows.shape[2]
    slots = n * cap
    chunks = points // LANES
    hcols = features // n
    packed = (n, 4 * cap, features // 2)
    vmem = pl.BlockSpec(memory_space=pltpu.VMEM)
    return pl.pallas_call(
        functools.partial(kernel, n, m),
        out_shape=(
            jax.ShapeDtypeStruct((1, points, features), BF16),
            jax.ShapeDtypeStruct(mesh_node_keys.shape, BF16),
            jax.ShapeDtypeStruct(mesh_node_values.shape, BF16),
            jax.ShapeDtypeStruct((1, hcols, nvar), F32),
        ),
        in_specs=[vmem] * 12,
        out_specs=(vmem,) * 4,
        scratch_shapes=[
            pltpu.VMEM(packed, BF16),
            pltpu.VMEM(packed, BF16),
            pltpu.VMEM(packed, BF16),
            pltpu.VMEM(packed, BF16),
            pltpu.VMEM((chunks, vpad, LANES), BF16),
            pltpu.VMEM((chunks, m, vpad, LANES), BF16),
            pltpu.VMEM((n, vpad, hcols), BF16),
            pltpu.VMEM((n, vpad, hcols), BF16),
            pltpu.VMEM((n, vpad, hcols), F32),
            pltpu.VMEM((points, features), BF16),
            pltpu.VMEM((vpad, features), BF16),
            pltpu.VMEM((2 * slots, features), F32),
            pltpu.VMEM((H * slots, features), BF16),
            pltpu.VMEM((H * slots, features), BF16),
            pltpu.VMEM((H * slots, features), BF16),
            pltpu.VMEM((K, H, points), F32),
            pltpu.VMEM((K, H, points), F32),
            pltpu.VMEM((H * slots, points), BF16),
            pltpu.VMEM((H * slots, points), BF16),
            pltpu.VMEM((H * slots, points), BF16),
            pltpu.VMEM((points, features), F32),
            pltpu.VMEM((points, features), BF16),
            pltpu.VMEM((vpad, points), F32),
            pltpu.VMEM((vpad, points), BF16),
            pltpu.VMEM((points, features), F32),
            pltpu.VMEM((points, features), BF16),
            pltpu.SemaphoreType.DMA((2, n)),
            pltpu.SemaphoreType.DMA((2, n)),
            pltpu.SemaphoreType.DMA((2, chunks, m)),
            pltpu.SemaphoreType.DMA((2, n)),
        ],
        compiler_params=pltpu.CompilerParams(
            collective_id=0, has_side_effects=True, vmem_limit_bytes=56 * 1024 * 1024
        ),
    )(
        grid_hidden_state,
        mesh_node_keys,
        mesh_node_values,
        query_weight,
        head_weight,
        rms_norm_gain.reshape(1, features),
        edge_bias,
        send_rows,
        edge_src,
        targets,
        point_area_weight.reshape(1, points),
        variable_loss_weight.reshape(1, nvar),
    )


def solution(mesh):
    placed = (
        P(("rep", "mem"), "grid", None),
        P(("rep", "mem"), "grid", None),
        P(("rep", "mem"), "grid", None),
        P(),
        P(),
        P(),
        P(None, None, "grid"),
        P("grid", None, None),
        P(None, "grid"),
        P("rep", "grid"),
        P("grid"),
        P(),
    )
    return jax.shard_map(
        shards,
        mesh=mesh,
        in_specs=placed,
        out_specs=(P(("rep", "mem"), "grid", None),) * 4,
        check_vma=False,
    )
```

```python
import functools
import math

import jax
import jax.numpy as jnp
from jax import lax
from jax.experimental import pallas as pl
from jax.experimental.pallas import tpu as pltpu
from jax.sharding import PartitionSpec as P

H = 16
K = 3
TAU = 0.1
EPS = 1e-06
LANES = 128
F32 = jnp.float32
BF16 = jnp.bfloat16
MESH = pl.DeviceIdType.MESH


def phi(value):
    return value * lax.rsqrt(value * value + TAU * TAU)


def mm(a, b, ca=1, cb=0):
    return lax.dot_general(a, b, (((ca,), (cb,)), ((), ())), preferred_element_type=F32)


def iota(shape, axis):
    return lax.broadcasted_iota(jnp.int32, shape, axis)


def ring_copies(src, dst, send_sem, recv_sem, axis, me, count):
    copies = []
    for step in range(1, count):
        peer = lax.rem(me + step, count)
        copies.append(
            pltpu.make_async_remote_copy(
                src_ref=src(peer),
                dst_ref=dst(me),
                send_sem=send_sem.at[step],
                recv_sem=recv_sem.at[step],
                device_id={axis: peer},
                device_id_type=MESH,
            )
        )
    return copies


def kernel(
    n,
    m,
    hidden_in,
    keys,
    values,
    wq_in,
    hw,
    gain_ref,
    bias,
    send_rows,
    edge_src,
    targets,
    area,
    var_weight,
    out_latent,
    out_returned,
    out_picks,
    out_head,
    hidden,
    wq,
    latent,
    local_sems,
    kv_send,
    kv_recv,
    back_send,
    back_recv,
    f_send,
    f_recv,
    hw_send,
    hw_recv,
    hw_own,
    q_ref,
    hwt,
    rows_ref,
    kb,
    vb,
    kbw,
    score_ref,
    w_ref,
    p_hi,
    p_lo,
    gs_ref,
    combined_ref,
    normed_ref,
    f_ref,
    pg_ref,
    gc_ref,
    gcb_ref,
    kv_sems,
    back_sems,
    f_sems,
    hw_sems,
):
    me = lax.axis_index("grid")
    member = lax.axis_index("mem")
    points, features = hidden.shape[1], hidden.shape[2]
    head = features // H
    per_tile = LANES // head
    cap = send_rows.shape[2]
    pair = 2 * cap
    slots = n * cap
    rows = n * pair
    half = features // 2
    nvar = hw.shape[0]
    vpad = hwt.shape[0]
    mesh_rows = keys.shape[1]
    chunks = points // LANES
    hcols = features // n

    barrier = pltpu.get_barrier_semaphore()
    for step in range(1, n):
        pl.semaphore_signal(
            barrier, inc=1, device_id={"grid": lax.rem(me + step, n)}, device_id_type=MESH
        )
    for step in range(1, m):
        pl.semaphore_signal(
            barrier, inc=1, device_id={"mem": lax.rem(member + step, m)}, device_id_type=MESH
        )
    load_hidden = pltpu.make_async_copy(hidden_in, hidden, local_sems.at[0])
    load_wq = pltpu.make_async_copy(wq_in, wq, local_sems.at[1])
    load_hidden.start()
    load_wq.start()

    table = send_rows[0].astype(F32).astype(BF16)
    spread_rows = jnp.where(iota((rows, n), 0) // pair == iota((rows, n), 1), 1.0, 0.0).astype(BF16)
    picked = mm(spread_rows, table)
    column = iota((rows, cap), 0) % cap == iota((rows, cap), 1)
    flat = jnp.sum(jnp.where(column, picked, 0.0), axis=1, keepdims=True)
    hit = iota((rows, mesh_rows), 1).astype(F32) == flat
    is_key = iota((rows, mesh_rows), 0) % pair < cap
    pick_key = jnp.where(hit & is_key, 1.0, 0.0).astype(BF16)
    pick_value = jnp.where(hit & ~is_key, 1.0, 0.0).astype(BF16)
    gathered = mm(pick_key, keys[0]) + mm(pick_value, values[0])

    def pack(block):
        return jnp.concatenate([block[:, :half], block[:, half:]], axis=0).astype(BF16)

    for d in range(n):
        kv_send[d] = pack(gathered[d * pair : (d + 1) * pair])

    pl.semaphore_wait(barrier, n + m - 2)

    kv_copies = ring_copies(
        lambda peer: kv_send.at[peer],
        lambda mine: kv_recv.at[mine],
        kv_sems.at[0],
        kv_sems.at[1],
        "grid",
        me,
        n,
    )
    for copy in kv_copies:
        copy.start()
    kv_recv[me] = kv_send[me]

    hwt[...] = jnp.zeros_like(hwt)
    hwt[:nvar, :] = hw[...]
    kb[...] = jnp.zeros_like(kb)
    vb[...] = jnp.zeros_like(vb)
    gain = gain_ref[...]
    area_row = area[...].reshape(1, points)
    out_picks[...] = jnp.concatenate([pick_key, pick_value], axis=0)
    vw = jnp.sum(
        jnp.where(iota((vpad, nvar), 0) == iota((vpad, nvar), 1), var_weight[...], 0.0),
        axis=1,
        keepdims=True,
    )

    load_hidden.wait()
    load_wq.wait()
    q_ref[...] = mm(hidden[0], wq[...]).astype(BF16)

    for copy in kv_copies:
        copy.wait_recv()
    for s in range(n):
        block = kv_recv[s].astype(F32)
        rows_ref[s * pair : (s + 1) * pair, :half] = block[:pair]
        rows_ref[s * pair : (s + 1) * pair, half:] = block[pair:]
    received = rows_ref[...].astype(BF16)
    slot_at = iota((slots, rows), 0)
    slot_row = slot_at // cap * pair + slot_at % cap
    at_key = jnp.where(iota((slots, rows), 1) == slot_row, 1.0, 0.0).astype(BF16)
    at_value = jnp.where(iota((slots, rows), 1) == slot_row + cap, 1.0, 0.0).astype(BF16)
    slot_k = mm(at_key, received)
    slot_v = mm(at_value, received)
    which = iota((slots, LANES), 1) // head
    for h in range(H):
        tile = slice(h // per_tile * LANES, (h // per_tile + 1) * LANES)
        mine = which == h % per_tile
        kb[h * slots : (h + 1) * slots, tile] = jnp.where(mine, slot_k[:, tile], 0.0).astype(BF16)
        vb[h * slots : (h + 1) * slots, tile] = jnp.where(mine, slot_v[:, tile], 0.0).astype(BF16)

    def onehots(at):
        slot = iota((slots, LANES), 0)
        return [slot == edge_src[k : k + 1, at] for k in range(K)]

    def select(table, hots, at):
        for h in range(H):
            part = table[h * slots : (h + 1) * slots]
            for k in range(K):
                score_ref[k, h : h + 1, at] = jnp.sum(
                    jnp.where(hots[k], part, 0.0), axis=0, keepdims=True
                )

    scale = 1.0 / math.sqrt(head)
    inverse = []
    f_copies = []
    for c in range(chunks):
        at = slice(c * LANES, (c + 1) * LANES)
        hots = onehots(at)
        select(mm(kb[...], q_ref[at, :], 1, 1), hots, at)
        scores = [score_ref[k, :, at] * scale + bias[k, :, at] for k in range(K)]
        top = functools.reduce(jnp.maximum, scores)
        exps = [jnp.exp(s - top) for s in scores]
        total = functools.reduce(jnp.add, exps)
        for k in range(K):
            w_ref[k, :, at] = exps[k] / total
        for h in range(H):
            block = functools.reduce(
                jnp.add,
                [jnp.where(hots[k], w_ref[k, h : h + 1, at], 0.0) for k in range(K)],
            )
            high = block.astype(BF16)
            p_hi[h * slots : (h + 1) * slots, at] = high
            p_lo[h * slots : (h + 1) * slots, at] = (block - high.astype(F32)).astype(BF16)
        attended = mm(p_hi[:, at], vb[...], 0, 0) + mm(p_lo[:, at], vb[...], 0, 0)
        combined = hidden[0, at, :].astype(F32) + attended
        inv = lax.rsqrt(jnp.mean(combined * combined, axis=1, keepdims=True) + EPS)
        inverse.append(inv)
        combined_ref[at, :] = combined
        normed_ref[at, :] = (combined * inv * gain).astype(BF16)
        forecast = mm(hwt[...], normed_ref[at, :], 1, 1)
        f_ref[:, at] = forecast
        f_send[c] = forecast.astype(BF16)
        copies = ring_copies(
            lambda peer, c=c: f_send.at[c],
            lambda mine, c=c: f_recv.at[c, mine],
            f_sems.at[0, c],
            f_sems.at[1, c],
            "mem",
            member,
            m,
        )
        for copy in copies:
            copy.start()
        f_copies.append(copies)

    kbw[...] = mm(kb[...], wq[...], 1, 1).astype(BF16)

    for c in range(chunks):
        at = slice(c * LANES, (c + 1) * LANES)
        for copy in f_copies[c]:
            copy.wait_recv()
        forecast = f_ref[:, at]
        pairwise = jnp.zeros_like(forecast)
        for step in range(1, m):
            other = f_recv[c, lax.rem(member + step, m)].astype(F32)
            pairwise = pairwise + phi(forecast - other)
        pairwise = pairwise[:nvar]
        spread = phi(forecast[:nvar] - targets[:, at]) / m - pairwise / (m * (m - 1))
        pg_ref[:nvar, at] = (area_row[:, at] * vw[:nvar] * spread).astype(BF16)
        pg_ref[nvar:, at] = jnp.zeros((vpad - nvar, LANES), BF16)

    head_part = mm(pg_ref[...], normed_ref[...]) * (1.0 / math.sqrt(points * n))
    for d in range(n):
        part = head_part[:, d * hcols : (d + 1) * hcols]
        hw_own[d] = part
        hw_send[d] = part.astype(BF16)
    hw_copies = ring_copies(
        lambda peer: hw_send.at[peer],
        lambda mine: hw_recv.at[mine],
        hw_sems.at[0],
        hw_sems.at[1],
        "grid",
        me,
        n,
    )
    for copy in hw_copies:
        copy.start()

    for c in range(chunks):
        at = slice(c * LANES, (c + 1) * LANES)
        hots = onehots(at)
        inv = inverse[c]
        combined = combined_ref[at, :]
        gained = mm(pg_ref[:, at], hwt[...], 0, 0) * gain
        along = jnp.mean(gained * combined, axis=1, keepdims=True)
        grad = inv * gained - combined * (inv * inv * inv * along)
        gc_ref[at, :] = grad
        gcb_ref[at, :] = grad.astype(BF16)
        select(mm(vb[...], gcb_ref[at, :], 1, 1), hots, at)
        grads = [score_ref[k, :, at] for k in range(K)]
        ws = [w_ref[k, :, at] for k in range(K)]
        centre = functools.reduce(jnp.add, [w * g for w, g in zip(ws, grads)])
        for k in range(K):
            score_ref[k, :, at] = ws[k] * (grads[k] - centre) * scale
        for h in range(H):
            block = functools.reduce(
                jnp.add,
                [jnp.where(hots[k], score_ref[k, h : h + 1, at], 0.0) for k in range(K)],
            )
            gs_ref[h * slots : (h + 1) * slots, at] = block.astype(BF16)

    slot_k_grad = mm(gs_ref[...], q_ref[...])
    slot_v_grad = mm(p_hi[...], gcb_ref[...])

    def own_heads(table):
        tiles = []
        for t in range(features // LANES):
            tile = slice(t * LANES, (t + 1) * LANES)
            value = None
            for i in range(per_tile):
                h = t * per_tile + i
                part = table[h * slots : (h + 1) * slots, tile]
                value = part if value is None else jnp.where(which == i, part, value)
            tiles.append(value)
        return jnp.concatenate(tiles, axis=1).astype(BF16)

    back = mm(at_key, own_heads(slot_k_grad), 0, 0) + mm(at_value, own_heads(slot_v_grad), 0, 0)
    for d in range(n):
        back_send[d] = pack(back[d * pair : (d + 1) * pair])
    back_copies = ring_copies(
        lambda peer: back_send.at[peer],
        lambda mine: back_recv.at[mine],
        back_sems.at[0],
        back_sems.at[1],
        "grid",
        me,
        n,
    )
    for copy in back_copies:
        copy.start()
    back_recv[me] = back_send[me]

    for c in range(chunks):
        at = slice(c * LANES, (c + 1) * LANES)
        latent[0, at, :] = (gc_ref[at, :] + mm(gs_ref[:, at], kbw[...], 0, 0)).astype(BF16)

    store_latent = pltpu.make_async_copy(latent, out_latent, local_sems.at[2])
    store_latent.start()

    for copy in hw_copies:
        copy.wait_recv()
    total = hw_own[me]
    for step in range(1, n):
        total = total + hw_recv[lax.rem(me + step, n)].astype(F32)
    out_head[:, 0, :] = total[:nvar]

    for copy in back_copies:
        copy.wait_recv()
    for s in range(n):
        block = back_recv[s].astype(F32)
        rows_ref[s * pair : (s + 1) * pair, :half] = block[:pair]
        rows_ref[s * pair : (s + 1) * pair, half:] = block[pair:]
    out_returned[...] = rows_ref[...].astype(BF16)

    store_latent.wait()
    for copies in [kv_copies, hw_copies, back_copies] + f_copies:
        for copy in copies:
            copy.wait_send()


def finish(latent, returned, picks, head, out_latent, out_keys, out_values, out_head, sems):
    copies = [
        pltpu.make_async_copy(latent, out_latent, sems.at[0]),
        pltpu.make_async_copy(head, out_head, sems.at[1]),
    ]
    for copy in copies:
        copy.start()
    rows = returned.shape[0]
    out_keys[0] = mm(picks[:rows], returned[...], 0, 0).astype(BF16)
    out_values[0] = mm(picks[rows:], returned[...], 0, 0).astype(BF16)
    for copy in copies:
        copy.wait()


def shards(
    grid_hidden_state,
    mesh_node_keys,
    mesh_node_values,
    query_weight,
    head_weight,
    rms_norm_gain,
    edge_bias,
    send_rows,
    edge_src,
    targets,
    point_area_weight,
    variable_loss_weight,
):
    n = lax.axis_size("grid")
    m = lax.axis_size("mem")
    points, features = grid_hidden_state.shape[1:]
    nvar = head_weight.shape[1]
    mesh_rows = mesh_node_keys.shape[1]
    vpad = -(-nvar // 16) * 16
    cap = send_rows.shape[2]
    slots = n * cap
    chunks = points // LANES
    hcols = features // n
    packed = (n, 4 * cap, features // 2)
    vmem = pl.BlockSpec(memory_space=pltpu.VMEM)
    hbm = pl.BlockSpec(memory_space=pl.ANY)
    latent, returned, picks, head = pl.pallas_call(
        functools.partial(kernel, n, m),
        out_shape=(
            jax.ShapeDtypeStruct((1, points, features), BF16),
            jax.ShapeDtypeStruct((2 * n * cap, features), BF16),
            jax.ShapeDtypeStruct((4 * n * cap, mesh_rows), BF16),
            jax.ShapeDtypeStruct((nvar, 1, hcols), F32),
        ),
        in_specs=[hbm, vmem, vmem, hbm] + [vmem] * 8,
        out_specs=(hbm, vmem, vmem, vmem),
        scratch_shapes=[
            pltpu.VMEM((1, points, features), BF16),
            pltpu.VMEM(query_weight.shape, BF16),
            pltpu.VMEM((1, points, features), BF16),
            pltpu.SemaphoreType.DMA((3,)),
            pltpu.VMEM(packed, BF16),
            pltpu.VMEM(packed, BF16),
            pltpu.VMEM(packed, BF16),
            pltpu.VMEM(packed, BF16),
            pltpu.VMEM((chunks, vpad, LANES), BF16),
            pltpu.VMEM((chunks, m, vpad, LANES), BF16),
            pltpu.VMEM((n, vpad, hcols), BF16),
            pltpu.VMEM((n, vpad, hcols), BF16),
            pltpu.VMEM((n, vpad, hcols), F32),
            pltpu.VMEM((points, features), BF16),
            pltpu.VMEM((vpad, features), BF16),
            pltpu.VMEM((2 * slots, features), F32),
            pltpu.VMEM((H * slots, features), BF16),
            pltpu.VMEM((H * slots, features), BF16),
            pltpu.VMEM((H * slots, features), BF16),
            pltpu.VMEM((K, H, points), F32),
            pltpu.VMEM((K, H, points), F32),
            pltpu.VMEM((H * slots, points), BF16),
            pltpu.VMEM((H * slots, points), BF16),
            pltpu.VMEM((H * slots, points), BF16),
            pltpu.VMEM((points, features), F32),
            pltpu.VMEM((points, features), BF16),
            pltpu.VMEM((vpad, points), F32),
            pltpu.VMEM((vpad, points), BF16),
            pltpu.VMEM((points, features), F32),
            pltpu.VMEM((points, features), BF16),
            pltpu.SemaphoreType.DMA((2, n)),
            pltpu.SemaphoreType.DMA((2, n)),
            pltpu.SemaphoreType.DMA((2, chunks, m)),
            pltpu.SemaphoreType.DMA((2, n)),
        ],
        compiler_params=pltpu.CompilerParams(
            collective_id=0, has_side_effects=True, vmem_limit_bytes=56 * 1024 * 1024
        ),
    )(
        grid_hidden_state,
        mesh_node_keys,
        mesh_node_values,
        query_weight,
        head_weight.T,
        rms_norm_gain.reshape(1, features),
        edge_bias,
        send_rows,
        edge_src,
        targets,
        point_area_weight,
        variable_loss_weight.reshape(1, nvar),
    )
    latent, key_grad, value_grad, head = pl.pallas_call(
        finish,
        out_shape=(
            jax.ShapeDtypeStruct((1, points, features), BF16),
            jax.ShapeDtypeStruct(mesh_node_keys.shape, BF16),
            jax.ShapeDtypeStruct(mesh_node_values.shape, BF16),
            jax.ShapeDtypeStruct((nvar, 1, hcols), F32),
        ),
        in_specs=[hbm, vmem, vmem, hbm],
        out_specs=(vmem,) * 4,
        scratch_shapes=[pltpu.SemaphoreType.DMA((2,))],
        compiler_params=pltpu.CompilerParams(vmem_limit_bytes=56 * 1024 * 1024),
    )(latent, returned, picks, head)
    return latent, key_grad, value_grad, jnp.transpose(head, (1, 2, 0))


def solution(mesh):
    placed = (
        P(("rep", "mem"), "grid", None),
        P(("rep", "mem"), "grid", None),
        P(("rep", "mem"), "grid", None),
        P(),
        P(),
        P(),
        P(None, None, "grid"),
        P("grid", None, None),
        P(None, "grid"),
        P("rep", "grid"),
        P("grid"),
        P(),
    )
    return jax.shard_map(
        shards,
        mesh=mesh,
        in_specs=placed,
        out_specs=(P(("rep", "mem"), "grid", None),) * 4,
        check_vma=False,
    )
```

```python
import functools
import math

import jax
import jax.numpy as jnp
from jax import lax
from jax.experimental import pallas as pl
from jax.experimental.pallas import tpu as pltpu
from jax.sharding import PartitionSpec as P

H = 16
K = 3
TAU = 0.1
EPS = 1e-06
LANES = 128
F32 = jnp.float32
BF16 = jnp.bfloat16
MESH = pl.DeviceIdType.MESH


def phi(value):
    return value * lax.rsqrt(value * value + TAU * TAU)


def mm(a, b, ca=1, cb=0):
    return lax.dot_general(a, b, (((ca,), (cb,)), ((), ())), preferred_element_type=F32)


def iota(shape, axis):
    return lax.broadcasted_iota(jnp.int32, shape, axis)


def ring_copies(src, dst, send_sem, recv_sem, axis, me, count):
    copies = []
    for step in range(1, count):
        peer = lax.rem(me + step, count)
        copies.append(
            pltpu.make_async_remote_copy(
                src_ref=src(peer),
                dst_ref=dst(me),
                send_sem=send_sem.at[step],
                recv_sem=recv_sem.at[step],
                device_id={axis: peer},
                device_id_type=MESH,
            )
        )
    return copies


def kernel(
    n,
    m,
    hidden_in,
    keys_in,
    values_in,
    wq_in,
    hw_in,
    gain_in,
    bias_in,
    send_in,
    edge_in,
    targets_in,
    area_in,
    var_in,
    out_latent,
    out_returned,
    out_picks,
    out_head,
    hidden,
    keys,
    values,
    wq,
    hw,
    gain_ref,
    bias,
    send_rows,
    edge_src,
    targets,
    area,
    var_weight,
    latent,
    local_sems,
    kv_send,
    kv_recv,
    back_send,
    back_recv,
    f_send,
    f_recv,
    hw_send,
    hw_recv,
    hw_own,
    q_ref,
    hwt,
    rows_ref,
    kb,
    vb,
    kbw,
    score_ref,
    w_ref,
    p_hi,
    p_lo,
    gs_ref,
    combined_ref,
    normed_ref,
    f_ref,
    pg_ref,
    gc_ref,
    gcb_ref,
    kv_sems,
    back_sems,
    f_sems,
    hw_sems,
):
    me = lax.axis_index("grid")
    member = lax.axis_index("mem")
    points, features = hidden.shape[1], hidden.shape[2]
    head = features // H
    per_tile = LANES // head
    cap = send_rows.shape[2]
    pair = 2 * cap
    slots = n * cap
    rows = n * pair
    half = features // 2
    nvar = hw.shape[0]
    vpad = hwt.shape[0]
    mesh_rows = keys.shape[1]
    chunks = points // LANES
    hcols = features // n

    barrier = pltpu.get_barrier_semaphore()
    for step in range(1, n):
        pl.semaphore_signal(
            barrier, inc=1, device_id={"grid": lax.rem(me + step, n)}, device_id_type=MESH
        )
    for step in range(1, m):
        pl.semaphore_signal(
            barrier, inc=1, device_id={"mem": lax.rem(member + step, m)}, device_id_type=MESH
        )
    arrays = [
        (send_in, send_rows),
        (keys_in, keys),
        (values_in, values),
        (hidden_in, hidden),
        (wq_in, wq),
        (hw_in, hw),
        (gain_in, gain_ref),
        (edge_in, edge_src),
        (bias_in, bias),
        (targets_in, targets),
        (area_in, area),
        (var_in, var_weight),
    ]
    loads = [
        pltpu.make_async_copy(src, dst, local_sems.at[1 + i]) for i, (src, dst) in enumerate(arrays)
    ]
    for load in loads:
        load.start()
    for load in loads[:3]:
        load.wait()

    table = send_rows[0].astype(F32).astype(BF16)
    spread_rows = jnp.where(iota((rows, n), 0) // pair == iota((rows, n), 1), 1.0, 0.0).astype(BF16)
    picked = mm(spread_rows, table)
    column = iota((rows, cap), 0) % cap == iota((rows, cap), 1)
    flat = jnp.sum(jnp.where(column, picked, 0.0), axis=1, keepdims=True)
    hit = iota((rows, mesh_rows), 1).astype(F32) == flat
    is_key = iota((rows, mesh_rows), 0) % pair < cap
    pick_key = jnp.where(hit & is_key, 1.0, 0.0).astype(BF16)
    pick_value = jnp.where(hit & ~is_key, 1.0, 0.0).astype(BF16)
    gathered = mm(pick_key, keys[0]) + mm(pick_value, values[0])

    def pack(block):
        return jnp.concatenate([block[:, :half], block[:, half:]], axis=0).astype(BF16)

    for d in range(n):
        kv_send[d] = pack(gathered[d * pair : (d + 1) * pair])

    pl.semaphore_wait(barrier, n + m - 2)

    kv_copies = ring_copies(
        lambda peer: kv_send.at[peer],
        lambda mine: kv_recv.at[mine],
        kv_sems.at[0],
        kv_sems.at[1],
        "grid",
        me,
        n,
    )
    for copy in kv_copies:
        copy.start()
    kv_recv[me] = kv_send[me]

    for load in loads[3:]:
        load.wait()
    hwt[...] = jnp.zeros_like(hwt)
    hwt[:nvar, :] = hw[...]
    kb[...] = jnp.zeros_like(kb)
    vb[...] = jnp.zeros_like(vb)
    gain = gain_ref[...]
    area_row = area[...].reshape(1, points)
    out_picks[...] = jnp.concatenate([pick_key, pick_value], axis=0)
    vw = jnp.sum(
        jnp.where(iota((vpad, nvar), 0) == iota((vpad, nvar), 1), var_weight[...], 0.0),
        axis=1,
        keepdims=True,
    )

    q_ref[...] = mm(hidden[0], wq[...]).astype(BF16)

    for copy in kv_copies:
        copy.wait_recv()
    for s in range(n):
        block = kv_recv[s].astype(F32)
        rows_ref[s * pair : (s + 1) * pair, :half] = block[:pair]
        rows_ref[s * pair : (s + 1) * pair, half:] = block[pair:]
    received = rows_ref[...].astype(BF16)
    slot_at = iota((slots, rows), 0)
    slot_row = slot_at // cap * pair + slot_at % cap
    at_key = jnp.where(iota((slots, rows), 1) == slot_row, 1.0, 0.0).astype(BF16)
    at_value = jnp.where(iota((slots, rows), 1) == slot_row + cap, 1.0, 0.0).astype(BF16)
    slot_k = mm(at_key, received)
    slot_v = mm(at_value, received)
    which = iota((slots, LANES), 1) // head
    for h in range(H):
        tile = slice(h // per_tile * LANES, (h // per_tile + 1) * LANES)
        mine = which == h % per_tile
        kb[h * slots : (h + 1) * slots, tile] = jnp.where(mine, slot_k[:, tile], 0.0).astype(BF16)
        vb[h * slots : (h + 1) * slots, tile] = jnp.where(mine, slot_v[:, tile], 0.0).astype(BF16)

    def onehots(at):
        slot = iota((slots, LANES), 0)
        return [slot == edge_src[k : k + 1, at] for k in range(K)]

    def select(table, hots, at):
        for h in range(H):
            part = table[h * slots : (h + 1) * slots]
            for k in range(K):
                score_ref[k, h : h + 1, at] = jnp.sum(
                    jnp.where(hots[k], part, 0.0), axis=0, keepdims=True
                )

    scale = 1.0 / math.sqrt(head)
    inverse = []
    f_copies = []
    for c in range(chunks):
        at = slice(c * LANES, (c + 1) * LANES)
        hots = onehots(at)
        select(mm(kb[...], q_ref[at, :], 1, 1), hots, at)
        scores = [score_ref[k, :, at] * scale + bias[k, :, at] for k in range(K)]
        top = functools.reduce(jnp.maximum, scores)
        exps = [jnp.exp(s - top) for s in scores]
        total = functools.reduce(jnp.add, exps)
        for k in range(K):
            w_ref[k, :, at] = exps[k] / total
        for h in range(H):
            block = functools.reduce(
                jnp.add,
                [jnp.where(hots[k], w_ref[k, h : h + 1, at], 0.0) for k in range(K)],
            )
            high = block.astype(BF16)
            p_hi[h * slots : (h + 1) * slots, at] = high
            p_lo[h * slots : (h + 1) * slots, at] = (block - high.astype(F32)).astype(BF16)
        attended = mm(p_hi[:, at], vb[...], 0, 0) + mm(p_lo[:, at], vb[...], 0, 0)
        combined = hidden[0, at, :].astype(F32) + attended
        inv = lax.rsqrt(jnp.mean(combined * combined, axis=1, keepdims=True) + EPS)
        inverse.append(inv)
        combined_ref[at, :] = combined
        normed_ref[at, :] = (combined * inv * gain).astype(BF16)
        forecast = mm(hwt[...], normed_ref[at, :], 1, 1)
        f_ref[:, at] = forecast
        f_send[c] = forecast.astype(BF16)
        copies = ring_copies(
            lambda peer, c=c: f_send.at[c],
            lambda mine, c=c: f_recv.at[c, mine],
            f_sems.at[0, c],
            f_sems.at[1, c],
            "mem",
            member,
            m,
        )
        for copy in copies:
            copy.start()
        f_copies.append(copies)

    kbw[...] = mm(kb[...], wq[...], 1, 1).astype(BF16)

    for c in range(chunks):
        at = slice(c * LANES, (c + 1) * LANES)
        for copy in f_copies[c]:
            copy.wait_recv()
        forecast = f_ref[:, at]
        pairwise = jnp.zeros_like(forecast)
        for step in range(1, m):
            other = f_recv[c, lax.rem(member + step, m)].astype(F32)
            pairwise = pairwise + phi(forecast - other)
        pairwise = pairwise[:nvar]
        spread = phi(forecast[:nvar] - targets[:, at]) / m - pairwise / (m * (m - 1))
        pg_ref[:nvar, at] = (area_row[:, at] * vw[:nvar] * spread).astype(BF16)
        pg_ref[nvar:, at] = jnp.zeros((vpad - nvar, LANES), BF16)

    head_part = mm(pg_ref[...], normed_ref[...]) * (1.0 / math.sqrt(points * n))
    for d in range(n):
        part = head_part[:, d * hcols : (d + 1) * hcols]
        hw_own[d] = part
        hw_send[d] = part.astype(BF16)
    hw_copies = ring_copies(
        lambda peer: hw_send.at[peer],
        lambda mine: hw_recv.at[mine],
        hw_sems.at[0],
        hw_sems.at[1],
        "grid",
        me,
        n,
    )
    for copy in hw_copies:
        copy.start()

    for c in range(chunks):
        at = slice(c * LANES, (c + 1) * LANES)
        hots = onehots(at)
        inv = inverse[c]
        combined = combined_ref[at, :]
        gained = mm(pg_ref[:, at], hwt[...], 0, 0) * gain
        along = jnp.mean(gained * combined, axis=1, keepdims=True)
        grad = inv * gained - combined * (inv * inv * inv * along)
        gc_ref[at, :] = grad
        gcb_ref[at, :] = grad.astype(BF16)
        select(mm(vb[...], gcb_ref[at, :], 1, 1), hots, at)
        grads = [score_ref[k, :, at] for k in range(K)]
        ws = [w_ref[k, :, at] for k in range(K)]
        centre = functools.reduce(jnp.add, [w * g for w, g in zip(ws, grads)])
        for k in range(K):
            score_ref[k, :, at] = ws[k] * (grads[k] - centre) * scale
        for h in range(H):
            block = functools.reduce(
                jnp.add,
                [jnp.where(hots[k], score_ref[k, h : h + 1, at], 0.0) for k in range(K)],
            )
            gs_ref[h * slots : (h + 1) * slots, at] = block.astype(BF16)

    slot_k_grad = mm(gs_ref[...], q_ref[...])
    slot_v_grad = mm(p_hi[...], gcb_ref[...])

    def own_heads(table):
        tiles = []
        for t in range(features // LANES):
            tile = slice(t * LANES, (t + 1) * LANES)
            value = None
            for i in range(per_tile):
                h = t * per_tile + i
                part = table[h * slots : (h + 1) * slots, tile]
                value = part if value is None else jnp.where(which == i, part, value)
            tiles.append(value)
        return jnp.concatenate(tiles, axis=1).astype(BF16)

    back = mm(at_key, own_heads(slot_k_grad), 0, 0) + mm(at_value, own_heads(slot_v_grad), 0, 0)
    for d in range(n):
        back_send[d] = pack(back[d * pair : (d + 1) * pair])
    back_copies = ring_copies(
        lambda peer: back_send.at[peer],
        lambda mine: back_recv.at[mine],
        back_sems.at[0],
        back_sems.at[1],
        "grid",
        me,
        n,
    )
    for copy in back_copies:
        copy.start()
    back_recv[me] = back_send[me]

    for c in range(chunks):
        at = slice(c * LANES, (c + 1) * LANES)
        latent[0, at, :] = (gc_ref[at, :] + mm(gs_ref[:, at], kbw[...], 0, 0)).astype(BF16)

    store_latent = pltpu.make_async_copy(latent, out_latent, local_sems.at[0])
    store_latent.start()

    for copy in hw_copies:
        copy.wait_recv()
    total = hw_own[me]
    for step in range(1, n):
        total = total + hw_recv[lax.rem(me + step, n)].astype(F32)
    out_head[:, 0, :] = total[:nvar]

    for copy in back_copies:
        copy.wait_recv()
    for s in range(n):
        block = back_recv[s].astype(F32)
        rows_ref[s * pair : (s + 1) * pair, :half] = block[:pair]
        rows_ref[s * pair : (s + 1) * pair, half:] = block[pair:]
    out_returned[...] = rows_ref[...].astype(BF16)

    store_latent.wait()
    for copies in [kv_copies, hw_copies, back_copies] + f_copies:
        for copy in copies:
            copy.wait_send()


def finish(
    latent, returned, picks, head, out_latent, out_keys, out_values, out_head, held, sems
):
    parts = held.shape[0]
    height = held.shape[1]
    loads, stores = [], []
    for i in range(parts):
        at = pl.ds(i * height, height)
        loads.append(pltpu.make_async_copy(latent.at[0, at], held.at[i], sems.at[0, i]))
        stores.append(pltpu.make_async_copy(held.at[i], out_latent.at[0, at], sems.at[1, i]))
    for load in loads:
        load.start()
    rows = returned.shape[0]
    out_keys[0] = mm(picks[:rows], returned[...], 0, 0).astype(BF16)
    out_values[0] = mm(picks[rows:], returned[...], 0, 0).astype(BF16)
    out_head[...] = head[...]
    for load, store in zip(loads, stores):
        load.wait()
        store.start()
    for store in stores:
        store.wait()


def shards(
    grid_hidden_state,
    mesh_node_keys,
    mesh_node_values,
    query_weight,
    head_weight,
    rms_norm_gain,
    edge_bias,
    send_rows,
    edge_src,
    targets,
    point_area_weight,
    variable_loss_weight,
):
    n = lax.axis_size("grid")
    m = lax.axis_size("mem")
    points, features = grid_hidden_state.shape[1:]
    nvar = head_weight.shape[1]
    mesh_rows = mesh_node_keys.shape[1]
    vpad = -(-nvar // 16) * 16
    cap = send_rows.shape[2]
    slots = n * cap
    chunks = points // LANES
    hcols = features // n
    packed = (n, 4 * cap, features // 2)
    vmem = pl.BlockSpec(memory_space=pltpu.VMEM)
    hbm = pl.BlockSpec(memory_space=pl.ANY)
    operands = (
        grid_hidden_state,
        mesh_node_keys,
        mesh_node_values,
        query_weight,
        head_weight.T,
        rms_norm_gain.reshape(1, features),
        edge_bias,
        send_rows,
        edge_src,
        targets,
        point_area_weight,
        variable_loss_weight.reshape(1, nvar),
    )
    latent, returned, picks, head = pl.pallas_call(
        functools.partial(kernel, n, m),
        out_shape=(
            jax.ShapeDtypeStruct((1, points, features), BF16),
            jax.ShapeDtypeStruct((2 * n * cap, features), BF16),
            jax.ShapeDtypeStruct((4 * n * cap, mesh_rows), BF16),
            jax.ShapeDtypeStruct((nvar, 1, hcols), F32),
        ),
        in_specs=[hbm] * 12,
        out_specs=(hbm, vmem, vmem, vmem),
        scratch_shapes=[
            *[pltpu.VMEM(a.shape, a.dtype) for a in operands],
            pltpu.VMEM((1, points, features), BF16),
            pltpu.SemaphoreType.DMA((1 + len(operands),)),
            pltpu.VMEM(packed, BF16),
            pltpu.VMEM(packed, BF16),
            pltpu.VMEM(packed, BF16),
            pltpu.VMEM(packed, BF16),
            pltpu.VMEM((chunks, vpad, LANES), BF16),
            pltpu.VMEM((chunks, m, vpad, LANES), BF16),
            pltpu.VMEM((n, vpad, hcols), BF16),
            pltpu.VMEM((n, vpad, hcols), BF16),
            pltpu.VMEM((n, vpad, hcols), F32),
            pltpu.VMEM((points, features), BF16),
            pltpu.VMEM((vpad, features), BF16),
            pltpu.VMEM((2 * slots, features), F32),
            pltpu.VMEM((H * slots, features), BF16),
            pltpu.VMEM((H * slots, features), BF16),
            pltpu.VMEM((H * slots, features), BF16),
            pltpu.VMEM((K, H, points), F32),
            pltpu.VMEM((K, H, points), F32),
            pltpu.VMEM((H * slots, points), BF16),
            pltpu.VMEM((H * slots, points), BF16),
            pltpu.VMEM((H * slots, points), BF16),
            pltpu.VMEM((points, features), F32),
            pltpu.VMEM((points, features), BF16),
            pltpu.VMEM((vpad, points), F32),
            pltpu.VMEM((vpad, points), BF16),
            pltpu.VMEM((points, features), F32),
            pltpu.VMEM((points, features), BF16),
            pltpu.SemaphoreType.DMA((2, n)),
            pltpu.SemaphoreType.DMA((2, n)),
            pltpu.SemaphoreType.DMA((2, chunks, m)),
            pltpu.SemaphoreType.DMA((2, n)),
        ],
        compiler_params=pltpu.CompilerParams(
            collective_id=0, has_side_effects=True, vmem_limit_bytes=56 * 1024 * 1024
        ),
    )(*operands)
    latent, key_grad, value_grad, head = pl.pallas_call(
        finish,
        out_shape=(
            jax.ShapeDtypeStruct((1, points, features), BF16),
            jax.ShapeDtypeStruct(mesh_node_keys.shape, BF16),
            jax.ShapeDtypeStruct(mesh_node_values.shape, BF16),
            jax.ShapeDtypeStruct((nvar, 1, hcols), F32),
        ),
        in_specs=[hbm, vmem, vmem, vmem],
        out_specs=(hbm, vmem, vmem, vmem),
        scratch_shapes=[
            pltpu.VMEM((chunks, LANES, features), BF16),
            pltpu.SemaphoreType.DMA((2, chunks)),
        ],
        compiler_params=pltpu.CompilerParams(vmem_limit_bytes=56 * 1024 * 1024),
    )(latent, returned, picks, head)
    return latent, key_grad, value_grad, jnp.transpose(head, (1, 2, 0))


def solution(mesh):
    placed = (
        P(("rep", "mem"), "grid", None),
        P(("rep", "mem"), "grid", None),
        P(("rep", "mem"), "grid", None),
        P(),
        P(),
        P(),
        P(None, None, "grid"),
        P("grid", None, None),
        P(None, "grid"),
        P("rep", "grid"),
        P("grid"),
        P(),
    )
    return jax.shard_map(
        shards,
        mesh=mesh,
        in_specs=placed,
        out_specs=(P(("rep", "mem"), "grid", None),) * 4,
        check_vma=False,
    )
```
